32 devices in a mesh: section: 2 (over core), patch: 4 (over y, x), req: 4 (over z).
Axes of the slice: x: 2, y: 2, z: 4, core: 2. Of those that a mesh axis runs over, the one named last changes fastest.
Arguments:
- hidden: bfloat16 [8, 1024, 1536], P('req', 'patch'), may hold values from -6 to 6
- w_qkv: bfloat16 [2, 1536, 2304], P('section', ('patch', 'req')), may hold values from -0.15625 to 0.15625
- w_out: bfloat16 [2, 768, 1536], P('section', ('patch', 'req')), may hold values from -0.21875 to 0.21875
- modulation: float32 [2, 8, 3, 1536], P('section', 'req'), may hold values from -3 to 3
- text_kv: bfloat16 [2, 8, 160, 1536], P('section', 'req'), may hold values from -1000 to 1000
- text_lengths: int32 [8], P('req'), may hold values from 77 to 154, as said below
- stale_kv: bfloat16 [2, 8, 1024, 1536], P('section', 'req', 'patch'), may hold values from -48 to 48
- held_hidden: bfloat16 [2, 8, 96, 1536], P('section', 'req', 'patch'), may hold values from -6 to 6
- recompute_rows: int32 [2, 8, 96], P('section', 'req', 'patch'), may hold values from 0 to 255, as said below
- coefficients: float32 [8, 2], P('req'), may hold values from 0.5 to 1.5
Outputs:
- latents: float32 [8, 1024, 1536], P('req', 'patch', 'section')
- cache: bfloat16 [2, 8, 1024, 1536], P('section', 'req', 'patch')
The draws below stay inside these ranges and needn't reach their ends.
Inputs may be any that keep to these rules, and one draw needn't show every extreme that they name: `text_lengths`: some request has exactly 154 text tokens and some exactly 77. `recompute_rows`: the row numbers listed for one layer, request and patch are distinct.
All inputs are finite; a program needn't handle non-finite values.
Results may differ from the reference program's by a relative error of at most 0.025.
Values may be sent and summed in bfloat16 or wider, within the bound.
A program may use at most 128 MiB of HBM per device.

```python
import jax
import jax.numpy as jnp
from jax import lax

D = 1536
HEAD = 64
HEADS = 12
PATCH_ROWS = 256
RECOMP = 24
TXT_MIN = 77
TXT_MAX = 154
PATCHES = 4
IMG = 1024
HK = 768
TXT = 160
REQUESTS = 8


def draw_text_kv(key, part):
    base = jax.random.normal(jax.random.fold_in(key, 11), (2, REQUESTS, TXT, 2 * HEADS * HEAD), jnp.float32)
    return jnp.clip(base, -1000.0, 1000.0).astype(jnp.bfloat16)


def draw_text_lengths(key, part):
    drawn = jax.random.randint(jax.random.fold_in(key, 21), (REQUESTS,), TXT_MIN, TXT_MAX + 1)
    drawn = drawn.at[0].set(TXT_MAX)
    return drawn.at[REQUESTS - 1].set(TXT_MIN).astype(jnp.int32)


def draw_recompute_rows(key, part):
    group_keys = jax.random.split(jax.random.fold_in(key, 31), 2 * REQUESTS * PATCHES)
    picked = jax.vmap(lambda group_key: jax.random.permutation(group_key, PATCH_ROWS)[:RECOMP])(group_keys)
    return picked.reshape(2, REQUESTS, PATCHES * RECOMP).astype(jnp.int32)


def draw_stale_kv(key, part):
    shape_keys = (2, REQUESTS, IMG, HEADS * HEAD)
    key_part = jax.random.normal(jax.random.fold_in(key, 41), shape_keys, jnp.float32)
    value_part = 8.0 * jax.random.normal(jax.random.fold_in(key, 42), shape_keys, jnp.float32)
    key_part = jnp.clip(key_part, -6.0, 6.0)
    value_part = jnp.clip(value_part, -48.0, 48.0)
    return jnp.concatenate([key_part, value_part], axis=-1).astype(jnp.bfloat16)


def steps_of(own_key, extent, cuts, low, largest):
    loudness = 1.0
    for dim, blocks in cuts:
        steps = jax.random.uniform(jax.random.fold_in(jax.random.fold_in(own_key, 6), dim), (blocks,), jnp.float32, low / len(cuts), largest / len(cuts))
        loudness = loudness * jnp.repeat(jnp.exp(steps), extent[dim] // blocks).reshape((-1,) + (1,) * (len(extent) - 1 - dim))
    return loudness


def scatter_about(rng, extent, width, bound, cuts=(), held_as=jnp.bfloat16):
    gain = steps_of(rng, extent, cuts, -0.22, 0.18) if cuts else 1.0
    result = jax.random.normal(rng, extent, jnp.float32) * width * gain
    return jnp.minimum(jnp.maximum(result, -bound), bound).astype(held_as)


def setup_inputs(seed: int = 0) -> dict:
    keys = jax.random.split(jax.random.key(seed), 11)
    return {
        "hidden": scatter_about(keys[0], (REQUESTS, IMG, D), 1.0, 6.0, ((0, 4), (1, 4))),
        "w_qkv": scatter_about(keys[1], (2, D, 3 * HK), D ** -0.5, 0.15625, ((0, 2), (1, 16))),
        "w_out": scatter_about(keys[2], (2, HK, D), HK ** -0.5, 0.21875, ((0, 2), (1, 16))),
        "modulation": scatter_about(keys[3], (2, REQUESTS, 3, D), 0.5, 3.0, ((0, 2), (1, 4)), jnp.float32),
        "text_kv": draw_text_kv(jax.random.fold_in(keys[10], 71), 0),
        "text_lengths": draw_text_lengths(jax.random.fold_in(keys[10], 71), 0),
        "stale_kv": draw_stale_kv(jax.random.fold_in(keys[10], 71), 0),
        "held_hidden": scatter_about(keys[7], (2, REQUESTS, PATCHES * RECOMP, D), 1.0, 6.0, ((0, 2), (1, 4), (2, 4))),
        "recompute_rows": draw_recompute_rows(jax.random.fold_in(keys[10], 71), 0),
        "coefficients": jnp.clip(0.5 + 1.0 * jax.random.uniform(keys[9], (REQUESTS, 2), jnp.float32) ** steps_of(keys[9], (REQUESTS, 2), ((0, 4),), -0.2, 0.2), 0.5, 1.5),
    }


norm_eps = 1e-06
score_scale = 0.125

def modulate(row_block, shift_row, scale_row):
    values = row_block.astype(jnp.float32)
    centre = values - lax.optimization_barrier(jnp.mean(values, axis=-1, keepdims=True))
    spread = lax.optimization_barrier(jnp.mean(centre * centre, axis=-1, keepdims=True))
    return (centre * lax.rsqrt(spread + norm_eps) * (1.0 + scale_row) + shift_row).astype(jnp.bfloat16)

def attend(queries, key_rows, value_rows, usable):
    row_count = queries.shape[0]
    feature_count = queries.shape[1]
    query_heads = queries.astype(jnp.float32).reshape(row_count, HEADS, feature_count // HEADS)
    key_heads = key_rows.astype(jnp.float32).reshape(key_rows.shape[0], HEADS, feature_count // HEADS)
    value_heads = value_rows.astype(jnp.float32).reshape(value_rows.shape[0], HEADS, feature_count // HEADS)
    scores = jnp.einsum('qhd,khd->hqk', query_heads, key_heads) * score_scale
    scores = jnp.where(usable[None, None, :], scores, -1e+30)
    row_max = lax.optimization_barrier(jnp.max(scores, axis=-1, keepdims=True))
    exp_scores = jnp.exp(scores - row_max)
    soft_weights = (exp_scores / lax.optimization_barrier(jnp.sum(exp_scores, axis=-1, keepdims=True))).astype(jnp.bfloat16)
    attended = jnp.einsum('hqk,khd->qhd', soft_weights.astype(jnp.float32), value_heads)
    return attended.reshape(row_count, feature_count).astype(jnp.bfloat16)

def run_layer(layer_input, mod_rows, qkv_weight, out_weight, text_rows, text_count, stale_block, held_rows, redo_index):
    head_width = out_weight.shape[0]
    held_norm = modulate(held_rows, mod_rows[0], mod_rows[1])
    redone = jnp.dot(held_norm, qkv_weight[:, head_width:], preferred_element_type=jnp.float32).astype(jnp.bfloat16)
    pieces = []
    for patch_number in range(PATCHES):
        stale_piece = stale_block[patch_number * PATCH_ROWS:(patch_number + 1) * PATCH_ROWS]
        first_row = patch_number * RECOMP
        pieces.append(stale_piece.at[redo_index[first_row:first_row + RECOMP]].set(redone[first_row:first_row + RECOMP]))
    normed = modulate(layer_input, mod_rows[0], mod_rows[1])
    projected = jnp.dot(normed, qkv_weight, preferred_element_type=jnp.float32).astype(jnp.bfloat16)
    fresh_all = projected[:, head_width:]
    usable = jnp.concatenate([jnp.arange(TXT) < text_count, jnp.ones((IMG,), jnp.bool_)])
    outputs = []
    for patch_number in range(PATCHES):
        row_start = patch_number * PATCH_ROWS
        image_rows = jnp.concatenate(pieces[:patch_number] + [fresh_all[row_start:row_start + PATCH_ROWS]] + pieces[patch_number + 1:], axis=0)
        context = jnp.concatenate([text_rows, image_rows], axis=0)
        attended = attend(projected[row_start:row_start + PATCH_ROWS, :head_width], context[:, :head_width], context[:, head_width:], usable)
        update = jnp.dot(attended, out_weight, preferred_element_type=jnp.float32)
        outputs.append((layer_input[row_start:row_start + PATCH_ROWS].astype(jnp.float32) + mod_rows[2] * update).astype(jnp.bfloat16))
    return (jnp.concatenate(outputs, axis=0), fresh_all)

def reference(hidden, w_qkv, w_out, modulation, text_kv, text_lengths, stale_kv, held_hidden, recompute_rows, coefficients):
    per_request = (hidden, jnp.moveaxis(modulation, 1, 0), jnp.moveaxis(text_kv, 1, 0), text_lengths, jnp.moveaxis(stale_kv, 1, 0), jnp.moveaxis(held_hidden, 1, 0), jnp.moveaxis(recompute_rows, 1, 0), coefficients)

    def one_request(bundle):
        source, mod_sets, text_sets, text_count, stales, held_sets, redo_sets, coef_pair = bundle
        layer_input = source
        caches = []
        for layer_index in range(2):
            layer_input, fresh_all = run_layer(layer_input, mod_sets[layer_index], w_qkv[layer_index], w_out[layer_index], text_sets[layer_index], text_count, stales[layer_index], held_sets[layer_index], redo_sets[layer_index])
            caches.append(fresh_all)
        latents = coef_pair[0] * source.astype(jnp.float32) + coef_pair[1] * layer_input.astype(jnp.float32)
        return (latents, jnp.stack(caches))
    latents, cache = lax.map(one_request, per_request)
    return (latents, jnp.moveaxis(cache, 1, 0))
```

```python
import functools

import jax
import jax.numpy as jnp
from jax import lax
from jax.experimental import pallas as pl
from jax.experimental.pallas import tpu as pltpu
from jax.sharding import PartitionSpec as P

HEADS = 12
norm_eps = 1e-06
score_scale = 0.125
MESH = pl.DeviceIdType.MESH


def shifted(block, axis, distance):
    devices = range(lax.axis_size(axis))
    route = [(i - distance, i) for i in devices if i - distance in devices]
    return lax.ppermute(block, axis, route)


def gather_kernel(
    nz, head_width, wq, wo, st, hd, rw, gq, go, gs, gh, gr, send_sems, recv_sems, local_sems
):
    c = lax.axis_index("section")
    p = lax.axis_index("patch")
    z = lax.axis_index("req")
    px = p + 1 - 2 * lax.rem(p, 2)
    py = lax.rem(p + 2, 4)
    pd = lax.rem(px + 2, 4)
    to_x, to_y, to_d = (c, px, z), (c, py, z), (c, pd, z)
    to_up, to_down = (c, p, z + 1), (c, p, z - 1)
    has_up, has_down = z < nz - 1, z > 0

    barrier = pltpu.get_barrier_semaphore()
    for device in (to_x, to_y, to_d):
        pl.semaphore_signal(barrier, inc=1, device_id=device, device_id_type=MESH)

    @pl.when(has_up)
    def _():
        pl.semaphore_signal(barrier, inc=1, device_id=to_up, device_id_type=MESH)

    @pl.when(has_down)
    def _():
        pl.semaphore_signal(barrier, inc=1, device_id=to_down, device_id_type=MESH)

    inner = jnp.logical_and(has_up, has_down)

    @pl.when(inner)
    def _():
        pl.semaphore_wait(barrier, 5)

    @pl.when(jnp.logical_not(inner))
    def _():
        pl.semaphore_wait(barrier, 4)

    count = [0]
    started = []

    def key():
        count[0] += 1
        return count[0] - 1

    def guarded(cond, run):
        if cond is None:
            run()
        else:
            pl.when(cond)(run)

    def copy(src, dst, k, device):
        return pltpu.make_async_remote_copy(
            src_ref=src,
            dst_ref=dst,
            send_sem=send_sems.at[k],
            recv_sem=recv_sems.at[k],
            device_id=device,
            device_id_type=MESH,
        )

    def start(src, dst, k, device, cond=None):
        guarded(cond, lambda: copy(src(), dst(), k, device).start())
        started.append((src, dst, k, device, cond))

    def arrive(ref, k, device, cond=None):
        guarded(cond, lambda: copy(ref(), ref(), k, device).wait_recv())

    qr, orows = wq.shape[0], wo.shape[0]
    full_width, out_width = wq.shape[1], wo.shape[1]

    def block_q(lo, hi):
        def at(patch, plane, half=None):
            first, width = lo, hi - lo
            if half is not None:
                width = width // 2
                first = lo + half * width
            row = pl.multiple_of((patch * nz + plane) * qr, qr)
            return gq.at[pl.ds(row, qr), pl.ds(first, width)]

        return at

    def block_o(patch, plane, half=None):
        first, width = 0, out_width
        if half is not None:
            width = width // 2
            first = half * width
        row = pl.multiple_of((patch * nz + plane) * orows, orows)
        return go.at[pl.ds(row, orows), pl.ds(first, width)]

    def block_s(request):
        def at(patch, plane, half=None):
            if half is None:
                return gs.at[patch, request]
            rows = st.shape[1] // 2
            return gs.at[patch, request, pl.ds(half * rows, rows)]

        return at

    class Plane:
        def __init__(self, at, plane, cond, own):
            self.at, self.plane, self.cond, self.own = at, plane, cond, own
            self.keys = [key() for _ in range(4)]

        def send(self):
            here = lambda: self.at(p, self.plane)
            start(self.own, here, self.keys[0], to_x, self.cond)
            start(self.own, here, self.keys[1], to_y, self.cond)

        def forward(self):
            at, plane = self.at, self.plane
            arrive(lambda: at(px, plane), self.keys[0], to_x, self.cond)
            first = lambda: at(px, plane, 0)
            start(first, first, self.keys[2], to_y, self.cond)
            arrive(lambda: at(py, plane), self.keys[1], to_y, self.cond)
            second = lambda: at(py, plane, 1)
            start(second, second, self.keys[3], to_x, self.cond)

        def finish(self):
            at, plane = self.at, self.plane
            arrive(lambda: at(pd, plane, 0), self.keys[2], to_y, self.cond)
            arrive(lambda: at(pd, plane, 1), self.keys[3], to_x, self.cond)

    block_k = block_q(head_width, full_width)
    firsts = [block_q(0, head_width), block_o]
    own_k = lambda: wq.at[:, pl.ds(head_width, full_width - head_width)]
    own_first = [lambda: wq.at[:, pl.ds(0, head_width)], lambda: wo]
    patches = (p, px, py, pd)
    up_k = [[[key() for _ in range(4)] for _ in range(nz)] for _ in range(2)]
    up_f = [[[key() for _ in range(2)] for _ in range(nz)] for _ in range(2)]
    lines = ((to_up, to_down, has_up, -1), (to_down, to_up, has_down, 1))

    def along(src, dst, keys, index, distance):
        for side, (target, _, present, _) in enumerate(lines):
            start(src, dst, keys[side][distance][index], target, present)

    plane_k = Plane(block_k, z, None, own_k)
    plane_k.send()
    along(own_k, lambda: block_k(p, z), up_k, 0, 1)
    own_planes = []
    for i in range(2):
        at = firsts[i]
        along(own_first[i], functools.partial(at, p, z), up_f, i, 1)
        own_planes.append(Plane(at, z, None, own_first[i]))
        own_planes[-1].send()
    small = []
    for src_ref, all_ref in ((hd, gh), (rw, gr)):
        for device, patch in ((to_x, px), (to_y, py), (to_d, pd)):
            k = key()
            start(lambda r=src_ref: r, lambda r=all_ref: r.at[p], k, device)
            small.append((lambda r=all_ref, q=patch: r.at[q], k, device))
    stale = [
        Plane(block_s(r), z, None, functools.partial(lambda n: st.at[n], r))
        for r in range(st.shape[0])
    ]
    for plane in stale:
        plane.send()
    local = [
        pltpu.make_async_copy(src, dst, local_sems.at[i])
        for i, (src, dst) in enumerate(
            (
                (wq, gq.at[pl.ds(pl.multiple_of((p * nz + z) * qr, qr), qr)]),
                (wo, block_o(p, z)),
                (st, gs.at[p]),
                (hd, gh.at[p]),
                (rw, gr.at[p]),
            )
        )
    ]
    for one in local:
        one.start()

    plane_k.forward()
    for i in (1, 2):
        ref = functools.partial(block_k, patches[i], z)
        along(ref, ref, up_k, i, 1)
    plane_k.finish()
    ref = functools.partial(block_k, pd, z)
    along(ref, ref, up_k, 3, 1)
    for plane in own_planes:
        plane.forward()

    pending = []
    waiting = list(stale)
    for d in range(1, nz):
        fresh_planes = []
        for side, (target, source, present, sign) in enumerate(lines):
            plane_z = z + sign * d
            cond = z >= d if sign < 0 else z < nz - d
            onward = jnp.logical_and(cond, present)
            for i in range(2):
                ref = functools.partial(firsts[i], p, plane_z)
                arrive(ref, up_f[side][d][i], source, cond)
                if d < nz - 1:
                    start(ref, ref, up_f[side][d + 1][i], target, onward)
                fresh_planes.append(Plane(firsts[i], plane_z, cond, ref))
                fresh_planes[-1].send()
        for i in range(4):
            for side, (target, source, present, sign) in enumerate(lines):
                plane_z = z + sign * d
                cond = z >= d if sign < 0 else z < nz - d
                onward = jnp.logical_and(cond, present)
                ref = functools.partial(block_k, patches[i], plane_z)
                arrive(ref, up_k[side][d][i], source, cond)
                if d < nz - 1:
                    start(ref, ref, up_k[side][d + 1][i], target, onward)
            if i == 1:
                for plane in fresh_planes:
                    plane.forward()
                if waiting:
                    one = waiting.pop(0)
                    one.forward()
                    pending.append(one)
        pending.extend(fresh_planes)
    for plane in waiting:
        plane.forward()
        pending.append(plane)
    for plane in own_planes + pending:
        plane.finish()
    for ref, k, device in small:
        arrive(ref, k, device)
    for one in local:
        one.wait()
    for src, dst, k, device, cond in started:
        guarded(cond, lambda s=src, t=dst, k=k, v=device: copy(s(), t(), k, v).wait_send())


def gather_all(w_qkv, w_out, stale, held, rows):
    nz = lax.axis_size("req")
    n_patch = lax.axis_size("patch")
    requests, recomp = rows.shape
    held_flat = held.reshape(-1, held.shape[-1])
    devices = nz * n_patch
    if n_patch != 4 or nz < 2 or nz > 4 or w_out.shape[0] % 16 or held_flat.shape[0] % 16:
        gq = lax.all_gather(w_qkv, ("patch", "req"), axis=0, tiled=True)
        go = lax.all_gather(w_out, ("patch", "req"), axis=0, tiled=True)
        gs = lax.all_gather(stale, "patch", axis=0)
        gh = lax.all_gather(held, "patch", axis=0)
        return gq, go, gs, gh, lax.all_gather(rows, "patch", axis=0)
    padded = jnp.pad(rows, ((0, -requests % 8), (0, -recomp % 128)))
    shapes = (
        jax.ShapeDtypeStruct((w_qkv.shape[0] * devices, w_qkv.shape[1]), w_qkv.dtype),
        jax.ShapeDtypeStruct((w_out.shape[0] * devices, w_out.shape[1]), w_out.dtype),
        jax.ShapeDtypeStruct((n_patch, *stale.shape), stale.dtype),
        jax.ShapeDtypeStruct((n_patch, *held_flat.shape), held.dtype),
        jax.ShapeDtypeStruct((n_patch, *padded.shape), rows.dtype),
    )
    sems = 4 + 12 * nz + 16 * nz + 4 * requests + 24
    gq, go, gs, gh, gr = pl.pallas_call(
        functools.partial(gather_kernel, nz, w_out.shape[0] * devices),
        out_shape=shapes,
        in_specs=[pl.BlockSpec(memory_space=pl.ANY)] * 5,
        out_specs=[pl.BlockSpec(memory_space=pl.ANY)] * 5,
        scratch_shapes=[
            pltpu.SemaphoreType.DMA((sems,)),
            pltpu.SemaphoreType.DMA((sems,)),
            pltpu.SemaphoreType.DMA((5,)),
        ],
        compiler_params=pltpu.CompilerParams(collective_id=0, has_side_effects=True),
        name="gather_all",
    )(w_qkv, w_out, stale, held_flat, padded)
    return gq, go, gs, gh.reshape(n_patch, *held.shape), gr[:, :requests, :recomp]


def modulate(row_block, mod):
    values = row_block.astype(jnp.float32)
    centre = values - jnp.mean(values, axis=-1, keepdims=True)
    spread = jnp.mean(centre * centre, axis=-1, keepdims=True)
    return (centre * lax.rsqrt(spread + norm_eps) * (1.0 + mod[1:2]) + mod[0:1]).astype(
        jnp.bfloat16
    )


def layer_kernel(
    lengths, x, wq, wo, mod, text, stale, held, rows, out, fresh, normed, projected, context, att
):
    request = pl.program_id(0)
    patch = lax.axis_index("patch")
    n_patch, patch_rows = stale.shape[0], stale.shape[2]
    head_width = wo.shape[0]
    text_slots = text.shape[1]
    redo = held.shape[1]
    image = n_patch * patch_rows
    head_size = head_width // HEADS
    f32 = jnp.float32

    mods = mod[0]
    normed[pl.ds(0, patch_rows), :] = modulate(x[0], mods)
    normed[pl.ds(patch_rows, redo), :] = modulate(held[0], mods)
    step = 256

    def project(i, carry):
        columns = pl.ds(pl.multiple_of(i * step, step), step)
        projected[:, columns] = jnp.dot(
            normed[...], wq[:, columns], preferred_element_type=f32
        ).astype(jnp.bfloat16)
        return carry

    lax.fori_loop(0, wq.shape[1] // step, project, 0)
    kv = pl.ds(head_width, 2 * head_width)
    row_of = lax.broadcasted_iota(jnp.int32, (patch_rows, redo), 0)
    slot_of = lax.broadcasted_iota(jnp.int32, (patch_rows, redo), 1)
    hit = row_of == rows[0]
    each = redo // n_patch
    for q in range(n_patch):
        pick = jnp.where(hit & (slot_of >= q * each) & (slot_of < (q + 1) * each), 1.0, 0.0)
        taken = jnp.sum(pick, axis=-1, keepdims=True) > 0.5
        moved = jnp.dot(
            pick.astype(jnp.bfloat16),
            projected[pl.ds(patch_rows, redo), kv],
            preferred_element_type=f32,
        )
        context[pl.ds(q * patch_rows, patch_rows), :] = jnp.where(
            taken, moved, stale[q, 0].astype(f32)
        ).astype(jnp.bfloat16)
    own = projected[pl.ds(0, patch_rows), kv]
    context[pl.ds(pl.multiple_of(patch * patch_rows, patch_rows), patch_rows), :] = own
    fresh[0] = own

    usable = lax.broadcasted_iota(jnp.int32, (1, text_slots), 1) < lengths[request]
    pair = 2 * head_size
    lane = lax.broadcasted_iota(jnp.int32, (patch_rows, pair), 1)

    def attend(i, carry):
        start = pl.multiple_of(i * pair, pair)
        keys = pl.ds(start, pair)
        values = pl.ds(pl.multiple_of(head_width + i * pair, pair), pair)
        queries = projected[pl.ds(0, patch_rows), keys] * jnp.asarray(score_scale, jnp.bfloat16)
        image_k, image_v = context[:, keys], context[:, values]
        text_k, text_v = text[0, :, keys], text[0, :, values]
        parts = []
        contract = (((1,), (1,)), ((), ()))
        for side in range(2):
            mine = (lane >= side * head_size) & (lane < (side + 1) * head_size)
            query = jnp.where(mine, queries, jnp.zeros_like(queries))
            s_image = lax.dot_general(query, image_k, contract, preferred_element_type=f32)
            s_text = lax.dot_general(query, text_k, contract, preferred_element_type=f32)
            s_text = jnp.where(usable, s_text, -1e30)
            top = jnp.maximum(
                jnp.max(s_image, axis=-1, keepdims=True), jnp.max(s_text, axis=-1, keepdims=True)
            )
            e_image, e_text = jnp.exp(s_image - top), jnp.exp(s_text - top)
            total = jnp.sum(e_image, axis=-1, keepdims=True) + jnp.sum(
                e_text, axis=-1, keepdims=True
            )
            mixed = jnp.dot(
                e_image.astype(jnp.bfloat16), image_v, preferred_element_type=f32
            ) + jnp.dot(e_text.astype(jnp.bfloat16), text_v, preferred_element_type=f32)
            parts.append(mixed / total)
        att[:, keys] = jnp.where(lane < head_size, parts[0], parts[1]).astype(jnp.bfloat16)
        return carry

    lax.fori_loop(0, HEADS // 2, attend, 0)

    def finish(i, carry):
        columns = pl.ds(pl.multiple_of(i * step, step), step)
        update = jnp.dot(att[...], wo[:, columns], preferred_element_type=f32)
        out[0, :, columns] = (
            x[0, :, columns].astype(f32) + mod[0, 2:3, columns] * update
        ).astype(jnp.bfloat16)
        return carry

    lax.fori_loop(0, wo.shape[1] // step, finish, 0)


def layer(x, wq, wo, mod, text, lengths, stale, held, rows):
    requests, patch_rows, width = x.shape
    n_patch = stale.shape[0]
    redo = held.shape[1]
    kv_width = 2 * wo.shape[0]
    one = lambda *shape: pl.BlockSpec((1, *shape), lambda r: (r,) + (0,) * len(shape))
    whole = lambda a: pl.BlockSpec(a.shape, lambda r: (0, 0), pipeline_mode=pl.Buffered(1))
    return pl.pallas_call(
        layer_kernel,
        grid=(requests,),
        out_shape=(
            jax.ShapeDtypeStruct(x.shape, jnp.bfloat16),
            jax.ShapeDtypeStruct((requests, patch_rows, kv_width), jnp.bfloat16),
        ),
        in_specs=[
            pl.BlockSpec(memory_space=pltpu.SMEM),
            one(patch_rows, width),
            whole(wq),
            whole(wo),
            one(*mod.shape[1:]),
            one(*text.shape[1:]),
            pl.BlockSpec((n_patch, 1, patch_rows, kv_width), lambda r: (0, r, 0, 0)),
            one(redo, width),
            one(1, redo),
        ],
        out_specs=(one(patch_rows, width), one(patch_rows, kv_width)),
        scratch_shapes=[
            pltpu.VMEM((patch_rows + redo, width), jnp.bfloat16),
            pltpu.VMEM((patch_rows + redo, wq.shape[1]), jnp.bfloat16),
            pltpu.VMEM((n_patch * patch_rows, kv_width), jnp.bfloat16),
            pltpu.VMEM((patch_rows, wo.shape[0]), jnp.bfloat16),
        ],
        compiler_params=pltpu.CompilerParams(vmem_limit_bytes=56 << 20),
        name="layer",
    )(lengths, x, wq, wo, mod, text, stale, held, rows)


def body(
    hidden,
    w_qkv,
    w_out,
    modulation,
    text_kv,
    text_lengths,
    stale_kv,
    held_hidden,
    recompute_rows,
    coefficients,
):
    section_index = lax.axis_index("section")
    model_width = hidden.shape[2]
    gq, go, gs, gh, gr = gather_all(
        w_qkv[0], w_out[0], stale_kv[0], held_hidden[0], recompute_rows[0]
    )
    requests = hidden.shape[0]
    held = jnp.swapaxes(gh, 0, 1).reshape(requests, -1, model_width)
    rows = jnp.swapaxes(gr, 0, 1).reshape(requests, 1, -1)

    def run(layer_input):
        return layer(
            layer_input, gq, go, modulation[0], text_kv[0], text_lengths, gs, held, rows
        )

    first_out, first_fresh = run(hidden)
    received = shifted(first_out, "section", 1)
    second_out, second_fresh = run(received)
    fresh_all = jnp.where(section_index == 0, first_fresh, second_fresh)
    half_width = model_width // 2
    returned = shifted(second_out[:, :, :half_width], "section", -1)
    own_half = jnp.where(section_index == 0, returned, second_out[:, :, half_width:])
    source_half = lax.dynamic_slice_in_dim(hidden, section_index * half_width, half_width, 2)
    latents = coefficients[:, 0][:, None, None] * source_half.astype(jnp.float32) + coefficients[
        :, 1
    ][:, None, None] * own_half.astype(jnp.float32)
    return (latents, fresh_all[None])


def solution(mesh):
    return jax.shard_map(
        body,
        mesh=mesh,
        in_specs=(
            P("req", "patch", None),
            P("section", ("patch", "req"), None),
            P("section", ("patch", "req"), None),
            P("section", "req", None, None),
            P("section", "req", None, None),
            P("req"),
            P("section", "req", "patch", None),
            P("section", "req", "patch", None),
            P("section", "req", "patch"),
            P("req", None),
        ),
        out_specs=(P("req", "patch", "section"), P("section", "req", "patch", None)),
        check_vma=False,
    )
```
